32 devices in a mesh: world: 2 (over x), gx: 16 (over z, y, core).
Axes of the slice: x: 2, y: 2, z: 4, core: 2. Of those that a mesh axis runs over, the one named last changes fastest.
Arguments:
- field: float32 [32, 256, 64, 128], P(None, ('world', 'gx')), parts along dimension 1, may hold values from -12 to 12
- occupancy: int32 [256, 64, 128], P(('world', 'gx')), parts along dimension 0, may hold values 0 or 1
- duals: float32 [64, 32], P('world'), parts along dimension 0, may hold values from -4 to 4
Outputs:
- field_out: float32 [32, 256, 64, 128], P(None, ('world', 'gx')), parts along dimension 1
- duals_out: float32 [64, 32], P('world'), parts along dimension 0
The draws below stay inside these ranges and needn't reach their ends.
There are 2 independent parts, one for each index of `world`. The reference program is written for one: setup_inputs(seed, part) draws one part's arguments, and reference() takes and returns one part's arrays. A program takes and returns all parts, laid end to end along the dimension named above; each array names one. Nothing has to cross between parts.
All inputs are finite; a program needn't handle non-finite values. No bound on the sum of `occupancy` on one device may be relied on, other than what follows from the above.
Results may differ from the reference program's by a relative error of at most 0.0001.
Values sent between devices are 32-bit elements; how exact they have to be, the bound alone decides.
A program may use at most 128 MiB of HBM per device.

```python
import jax
import jax.numpy as jnp
from jax import lax

K = 32
NY = 128
NZ = 64
ITERS = 2
NX = 128
NCELLS = 1048576


def draw_field(key, part):
    key = jax.random.fold_in(key, 7)
    xpos = jnp.arange(NX, dtype=jnp.float32) / NX
    ramp = (0.6 + 1.2 * xpos)[None, :, None, None]
    base = jax.random.normal(jax.random.fold_in(key, 1), (K, NX, NZ, NY), jnp.float32)
    values = jnp.clip(base, -5.0, 5.0) * ramp
    return values.astype(jnp.float32)


def with_ends(array, own_key, low, high):
    spot = [jax.random.randint(jax.random.fold_in(own_key, axis), (), 0, length) for axis, length in enumerate(array.shape)]
    longest = array.shape.index(max(array.shape))
    next_to = spot[:longest] + [(spot[longest] + 1) % array.shape[longest]] + spot[longest + 1:]
    return array.at[tuple(spot)].set(low).at[tuple(next_to)].set(high)


def scatter_about(own_key, shape, deviation, most, held_as=jnp.bfloat16):
    array = deviation * jax.random.normal(own_key, shape, jnp.float32)
    return jnp.clip(array, min=-most, max=most).astype(held_as)


def setup_inputs(seed: int = 0, part: int = 0) -> dict:
    seeds = jax.random.split(jax.random.key(seed), 4)
    own_keys = jax.random.split(jax.random.fold_in(seeds[3], part), 4)
    return {
        "field": draw_field(jax.random.fold_in(jax.random.fold_in(seeds[3], part), 71), part),
        "occupancy": with_ends((jax.random.randint(own_keys[1], (NX, NZ, NY), 0, 5) < 4).astype(jnp.int32), jax.random.fold_in(own_keys[1], 1), 0, 1),
        "duals": scatter_about(own_keys[2], (K, K), 1.0, 4.0, jnp.float32),
    }


def laplace(u, m):
    padded = jnp.pad(u, ((0, 0), (1, 1), (1, 1), (1, 1)))
    mpad = jnp.pad(m, 1)
    core = padded[:, 1:-1, 1:-1, 1:-1]
    mc = mpad[1:-1, 1:-1, 1:-1]
    total = jnp.zeros_like(u)
    shifts = [(2, 1, 1), (0, 1, 1), (1, 2, 1), (1, 0, 1), (1, 1, 2), (1, 1, 0)]
    for a, b, c in shifts:
        nb = padded[:, a:a + u.shape[1], b:b + u.shape[2], c:c + u.shape[3]]
        mn = mpad[a:a + u.shape[1], b:b + u.shape[2], c:c + u.shape[3]]
        total = total + (mc * mn)[None] * (core - nb)
    return total


def reference(field, occupancy, duals):
    m = occupancy.astype(jnp.float32)
    u = field
    beta = duals
    eye = jnp.eye(K, dtype=jnp.float32)
    for step in range(ITERS):
        gram_mat = jnp.einsum("kxzy,jxzy->kj", u * m[None], u, precision=lax.Precision.HIGHEST) / NCELLS
        qmat = jnp.tril(beta + 1.0 * (gram_mat - eye))
        mixed = jnp.einsum("kj,jxzy->kxzy", qmat, u, precision=lax.Precision.HIGHEST)
        u = u - 0.1 * (laplace(u, m) + m[None] * mixed)
        beta = beta + 0.5 * jnp.tril(gram_mat - eye)
    return u, beta
```

```python
import functools

import jax
import jax.numpy as jnp
from jax import lax
from jax.experimental import pallas as pl
from jax.experimental.pallas import tpu as pltpu
from jax.sharding import PartitionSpec as P

MESH = pl.DeviceIdType.MESH
HI = lax.Precision.HIGHEST
S8 = 8
F32 = jnp.float32
BF16 = jnp.bfloat16


def iota(shape, dim):
    return lax.broadcasted_iota(jnp.int32, shape, dim)


def dot_nt(a, b, precision=None):
    return lax.dot_general(a, b, (((1,), (1,)), ((), ())), precision=precision, preferred_element_type=F32)


def dot_nn(a, b, precision=None):
    return lax.dot_general(a, b, (((1,), (0,)), ((), ())), precision=precision, preferred_element_type=F32)


def split(x):
    high = x.astype(BF16)
    return high, (x - high.astype(F32)).astype(BF16)


def kernel(n, field, occ, duals, out, duals_out, u, v0, v1, parts, mask, keep, acc, mix, shift,
           gsend, gbuf, in_sem, out_sem, h_send, h_recv, m_send, m_recv, g_send, g_recv):
    me = lax.axis_index("gx")
    rows, channels, depth, across = u.shape
    wide = channels * S8
    groups = depth // S8
    count = n * rows * depth * across
    last = rows + 1

    barrier = pltpu.get_barrier_semaphore()

    def greet(d, c):
        pl.semaphore_signal(barrier, inc=1, device_id={"gx": lax.rem(me + d, n)}, device_id_type=MESH)
        return c

    lax.fori_loop(1, n, greet, 0)

    def fetch(x):
        return pltpu.make_async_copy(field.at[:, x], u.at[x], in_sem.at[x])

    fetch(0).start()
    fetch(rows - 1).start()
    for x in range(1, rows - 1):
        fetch(x).start()

    for x in range(rows):
        mask[x + 1] = occ[x].astype(F32)

    @pl.when(me == 0)
    def _():
        mask[0] = jnp.zeros((depth, across), F32)
        v0[0] = jnp.zeros((channels, depth, across), F32)
        v1[0] = jnp.zeros((channels, depth, across), F32)

    @pl.when(me == n - 1)
    def _():
        mask[last] = jnp.zeros((depth, across), F32)
        v0[last] = jnp.zeros((channels, depth, across), F32)
        v1[last] = jnp.zeros((channels, depth, across), F32)

    def to_left(src, dst, send, recv):
        return pltpu.make_async_remote_copy(src_ref=src, dst_ref=dst, send_sem=send, recv_sem=recv,
                                            device_id={"gx": me - 1}, device_id_type=MESH)

    def to_right(src, dst, send, recv):
        return pltpu.make_async_remote_copy(src_ref=src, dst_ref=dst, send_sem=send, recv_sem=recv,
                                            device_id={"gx": me + 1}, device_id_type=MESH)

    mask_l = to_left(mask.at[1], mask.at[last], m_send.at[0], m_recv.at[0])
    mask_r = to_right(mask.at[rows], mask.at[0], m_send.at[1], m_recv.at[1])
    u_l = to_left(u.at[0], v0.at[last], h_send.at[0], h_recv.at[0])
    u_r = to_right(u.at[rows - 1], v0.at[0], h_send.at[1], h_recv.at[1])
    w_l = to_left(v1.at[1], v1.at[last], h_send.at[2], h_recv.at[2])
    w_r = to_right(v1.at[rows], v1.at[0], h_send.at[3], h_recv.at[3])

    pl.semaphore_wait(barrier, n - 1)

    @pl.when(me > 0)
    def _():
        mask_l.start()

    @pl.when(me < n - 1)
    def _():
        mask_r.start()

    fetch(0).wait()

    @pl.when(me > 0)
    def _():
        u_l.start()

    fetch(rows - 1).wait()

    @pl.when(me < n - 1)
    def _():
        u_r.start()

    lane_shift = (jnp.abs(iota((across, across), 0) - iota((across, across), 1)) == 1).astype(F32).astype(BF16)
    shift[0:across] = lane_shift
    shift[across:2 * across] = lane_shift

    def spread(columns):
        return (iota((wide, columns), 0) // S8 == iota((wide, columns), 1)).astype(F32)

    def same_slot():
        return iota((wide, wide), 0) % S8 == iota((wide, wide), 1) % S8

    def store_parts(x, g, v):
        high, low = split(v.reshape(wide, across))
        parts[x, 0:wide, g * across:(g + 1) * across] = high
        parts[x, wide:2 * wide, g * across:(g + 1) * across] = low

    def add_gram(x):
        acc[...] += dot_nt(parts[x, 0:wide, :], parts[x])

    acc[...] = jnp.zeros_like(acc)

    def load_row(x, c):
        for g in range(groups):
            z = slice(g * S8, (g + 1) * S8)
            v = mask[x + 1, z][None] * u[x, :, z, :]
            v0[x + 1, :, z, :] = v
            store_parts(x, g, v)
        add_gram(x)
        return c

    def fetch_row(x, c):
        fetch(x).wait()
        return load_row(x, c)

    lax.fori_loop(1, rows - 1, fetch_row, 0)
    load_row(0, 0)
    load_row(rows - 1, 0)

    def gram_copy(r, d):
        return pltpu.make_async_remote_copy(
            src_ref=gsend.at[r], dst_ref=gbuf.at[r, d], send_sem=g_send.at[r, d], recv_sem=g_recv.at[r, d],
            device_id={"gx": lax.rem(me + d, n)}, device_id_type=MESH)

    def gram_start(r):
        same = same_slot()
        e_t = (iota((channels, wide), 0) == iota((channels, wide), 1) // S8).astype(F32)
        e = spread(across)
        hh = dot_nn(dot_nn(e_t, jnp.where(same, acc[:, 0:wide], 0.0), HI), e, HI)
        hl = dot_nn(dot_nn(e_t, jnp.where(same, acc[:, wide:2 * wide], 0.0), HI), e, HI)
        eye = (iota((channels, channels), 0) == iota((channels, channels), 1)).astype(F32)
        eye_wide = (iota((channels, across), 0) == iota((channels, across), 1)).astype(F32)
        lh = lax.dot_general(hl[:, 0:channels], eye_wide, (((0,), (0,)), ((), ())), precision=HI,
                             preferred_element_type=F32)
        gsend[r] = hh + hl + lh
        lax.fori_loop(1, n, lambda d, c: (gram_copy(r, d).start(), c)[1], 0)

    def gram_end(r):
        def body(d, c):
            gram_copy(r, d).wait()
            return c

        lax.fori_loop(1, n, body, 0)

        def add(d, total):
            return total + gbuf[r, d]

        total = lax.fori_loop(1, n, add, gsend[r])
        return total[:, 0:channels] / count

    def mixing(g, beta):
        row, col = iota((channels, channels), 0), iota((channels, channels), 1)
        low = row >= col
        excess = g - (row == col).astype(F32)
        q = jnp.where(low, beta + 1.0 * excess, 0.0)
        e = spread(channels)
        big = jnp.where(same_slot(), -dot_nt(dot_nn(e, q, HI), e, HI), 0.0)
        high, rest = split(big)
        mix[:, 0:wide] = high
        mix[:, wide:2 * wide] = high
        mix[:, 2 * wide:3 * wide] = rest
        return beta + 0.5 * jnp.where(low, excess, 0.0)

    sub = iota((1, S8, across), 1)

    def advance_row(v, x, write):
        zero = jnp.zeros((channels, S8, across), F32)
        pairs = 2
        for g0 in range(0, groups, pairs):
            cols = slice(g0 * across, (g0 + pairs) * across)
            mixed = dot_nn(mix[:, 0:2 * wide], parts[x, :, cols]) + dot_nn(mix[:, 2 * wide:], parts[x, 0:wide, cols])
            sides = []
            for g in range(g0, g0 + pairs):
                own = slice(g * across, (g + 1) * across)
                sides.append(dot_nn(parts[x, 0:wide, own], shift[0:across])
                             + dot_nn(parts[x, wide:2 * wide, own], shift[across:2 * across]))
            for i, g in enumerate(range(g0, g0 + pairs)):
                z = slice(g * S8, (g + 1) * S8)
                core = v[x + 1, :, z, :]
                before = v[x + 1, :, (g - 1) * S8:g * S8, :] if g > 0 else zero
                after = v[x + 1, :, (g + 1) * S8:(g + 2) * S8, :] if g < groups - 1 else zero
                up = pltpu.roll(jnp.where(sub == S8 - 1, before, core), 1, 1)
                down = pltpu.roll(jnp.where(sub == 0, after, core), S8 - 1, 1)
                total = (mixed[:, i * across:(i + 1) * across] + sides[i]).reshape(channels, S8, across)
                total = total + up + down + v[x, :, z, :] + v[x + 2, :, z, :]
                new = keep[x, z][None] * core + (0.1 * mask[x + 1, z])[None] * total
                write(x, g, z, new)

    def write_first(x, g, z, new):
        v1[x + 1, :, z, :] = new
        store_parts(x, g, new)

    def write_last(x, g, z, new):
        u[x, :, z, :] = jnp.where(mask[x + 1, z][None] > 0.5, new, u[x, :, z, :])

    gram_start(0)

    @pl.when(me > 0)
    def _():
        mask_r.wait_recv()

    @pl.when(me < n - 1)
    def _():
        mask_l.wait_recv()

    zi, yi = iota((depth, across), 0), iota((depth, across), 1)

    def weigh(x, c):
        m = mask[x + 1]
        near = mask[x] + mask[x + 2]
        near = near + jnp.where(yi == 0, 0.0, pltpu.roll(m, 1, 1))
        near = near + jnp.where(yi == across - 1, 0.0, pltpu.roll(m, across - 1, 1))
        near = near + jnp.where(zi == 0, 0.0, pltpu.roll(m, 1, 0))
        near = near + jnp.where(zi == depth - 1, 0.0, pltpu.roll(m, depth - 1, 0))
        keep[x] = m * (1.0 - 0.1 * near)
        return c

    lax.fori_loop(0, rows, weigh, 0)

    beta = mixing(gram_end(0), duals[...])
    acc[...] = jnp.zeros_like(acc)

    def first(x, c):
        advance_row(v0, x, write_first)
        add_gram(x)
        return c

    lax.fori_loop(1, rows - 1, first, 0)

    @pl.when(me > 0)
    def _():
        u_r.wait_recv()
        v0[0] = v0[0] * mask[0][None]

    first(0, 0)

    @pl.when(me > 0)
    def _():
        w_l.start()

    @pl.when(me < n - 1)
    def _():
        u_l.wait_recv()
        v0[last] = v0[last] * mask[last][None]

    first(rows - 1, 0)

    @pl.when(me < n - 1)
    def _():
        w_r.start()

    gram_start(1)
    beta = mixing(gram_end(1), beta)
    duals_out[...] = beta

    def store(x):
        return pltpu.make_async_copy(u.at[x], out.at[:, x], out_sem.at[x])

    def second(x, c):
        advance_row(v1, x, write_last)
        store(x).start()
        return c

    lax.fori_loop(1, rows - 1, second, 0)

    @pl.when(me > 0)
    def _():
        mask_l.wait_send()
        u_l.wait_send()
        w_r.wait_recv()

    @pl.when(me < n - 1)
    def _():
        mask_r.wait_send()
        u_r.wait_send()
        w_l.wait_recv()

    second(0, 0)
    second(rows - 1, 0)

    @pl.when(me > 0)
    def _():
        w_l.wait_send()

    @pl.when(me < n - 1)
    def _():
        w_r.wait_send()

    lax.fori_loop(0, rows, lambda x, c: (store(x).wait(), c)[1], 0)


def per_device(field, occupancy, duals):
    channels, rows, depth, across = field.shape
    n = lax.axis_size("gx")
    wide = channels * S8
    vmem = pl.BlockSpec(memory_space=pltpu.VMEM)
    dma = pltpu.SemaphoreType.DMA
    return pl.pallas_call(
        functools.partial(kernel, n),
        out_shape=(jax.ShapeDtypeStruct(field.shape, F32), jax.ShapeDtypeStruct(duals.shape, F32)),
        in_specs=[pl.BlockSpec(memory_space=pl.ANY), vmem, vmem],
        out_specs=(pl.BlockSpec(memory_space=pl.ANY), vmem),
        scratch_shapes=[
            pltpu.VMEM((rows, channels, depth, across), F32),
            pltpu.VMEM((rows + 2, channels, depth, across), F32),
            pltpu.VMEM((rows + 2, channels, depth, across), F32),
            pltpu.VMEM((rows, 2 * wide, depth // S8 * across), BF16),
            pltpu.VMEM((rows + 2, depth, across), F32),
            pltpu.VMEM((rows, depth, across), F32),
            pltpu.VMEM((wide, 2 * wide), F32),
            pltpu.VMEM((wide, 3 * wide), BF16),
            pltpu.VMEM((2 * across, across), BF16),
            pltpu.VMEM((2, channels, across), F32),
            pltpu.VMEM((2, n, channels, across), F32),
            dma((rows,)), dma((rows,)), dma((4,)), dma((4,)), dma((2,)), dma((2,)), dma((2, n)), dma((2, n)),
        ],
        compiler_params=pltpu.CompilerParams(
            collective_id=0, has_side_effects=True, vmem_limit_bytes=56 * 1024 * 1024),
    )(field, occupancy, duals)


def solution(mesh):
    placed = (
        P(None, ("world", "gx"), None, None),
        P(("world", "gx"), None, None),
        P("world", None),
    )
    return jax.shard_map(
        per_device,
        mesh=mesh,
        in_specs=placed,
        out_specs=(P(None, ("world", "gx"), None, None), P("world", None)),
        check_vma=False,
    )
```

```python
import functools

import jax
import jax.numpy as jnp
from jax import lax
from jax.experimental import pallas as pl
from jax.experimental.pallas import tpu as pltpu
from jax.sharding import PartitionSpec as P

MESH = pl.DeviceIdType.MESH
HI = lax.Precision.HIGHEST
S8 = 8
F32 = jnp.float32
BF16 = jnp.bfloat16


def iota(shape, dim):
    return lax.broadcasted_iota(jnp.int32, shape, dim)


def dot_nt(a, b, precision=None):
    return lax.dot_general(a, b, (((1,), (1,)), ((), ())), precision=precision, preferred_element_type=F32)


def dot_nn(a, b, precision=None):
    return lax.dot_general(a, b, (((1,), (0,)), ((), ())), precision=precision, preferred_element_type=F32)


def split(x):
    high = x.astype(BF16)
    return high, (x - high.astype(F32)).astype(BF16)


def kernel(n, field, occ, duals, out, duals_out, u, v0, v1, parts, mask, keep, acc, mix, shift,
           gsend, gbuf, in_sem, out_sem, h_send, h_recv, m_send, m_recv, g_send, g_recv):
    me = lax.axis_index("gx")
    rows, channels, depth, across = u.shape
    wide = channels * S8
    groups = depth // S8
    count = n * rows * depth * across
    last = rows + 1

    barrier = pltpu.get_barrier_semaphore()

    def greet(d, c):
        pl.semaphore_signal(barrier, inc=1, device_id={"gx": lax.rem(me + d, n)}, device_id_type=MESH)
        return c

    lax.fori_loop(1, n, greet, 0)

    def fetch(x):
        return pltpu.make_async_copy(field.at[:, x], u.at[x], in_sem.at[x])

    fetch(0).start()
    fetch(rows - 1).start()
    for x in range(1, rows - 1):
        fetch(x).start()

    for x in range(rows):
        mask[x + 1] = occ[x].astype(F32)

    @pl.when(me == 0)
    def _():
        mask[0] = jnp.zeros((depth, across), F32)
        v0[0] = jnp.zeros((channels, depth, across), F32)
        v1[0] = jnp.zeros((channels, depth, across), F32)

    @pl.when(me == n - 1)
    def _():
        mask[last] = jnp.zeros((depth, across), F32)
        v0[last] = jnp.zeros((channels, depth, across), F32)
        v1[last] = jnp.zeros((channels, depth, across), F32)

    def to_left(src, dst, send, recv):
        return pltpu.make_async_remote_copy(src_ref=src, dst_ref=dst, send_sem=send, recv_sem=recv,
                                            device_id={"gx": me - 1}, device_id_type=MESH)

    def to_right(src, dst, send, recv):
        return pltpu.make_async_remote_copy(src_ref=src, dst_ref=dst, send_sem=send, recv_sem=recv,
                                            device_id={"gx": me + 1}, device_id_type=MESH)

    mask_l = to_left(mask.at[1], mask.at[last], m_send.at[0], m_recv.at[0])
    mask_r = to_right(mask.at[rows], mask.at[0], m_send.at[1], m_recv.at[1])
    cut = channels * 3 // 8
    pieces = (pl.ds(0, cut), pl.ds(cut, channels - cut))
    u_l = [to_left(u.at[0, p], v0.at[last, p], h_send.at[i], h_recv.at[i]) for i, p in enumerate(pieces)]
    u_r = [to_right(u.at[rows - 1, p], v0.at[0, p], h_send.at[2 + i], h_recv.at[2 + i]) for i, p in enumerate(pieces)]
    w_l = to_left(v1.at[1], v1.at[last], h_send.at[4], h_recv.at[4])
    w_r = to_right(v1.at[rows], v1.at[0], h_send.at[5], h_recv.at[5])

    pl.semaphore_wait(barrier, n - 1)

    @pl.when(me > 0)
    def _():
        mask_l.start()

    @pl.when(me < n - 1)
    def _():
        mask_r.start()

    fetch(0).wait()

    @pl.when(me > 0)
    def _():
        u_l[0].start()

    fetch(rows - 1).wait()

    @pl.when(me < n - 1)
    def _():
        u_r[0].start()

    lane_shift = (jnp.abs(iota((across, across), 0) - iota((across, across), 1)) == 1).astype(F32).astype(BF16)
    shift[0:across] = lane_shift
    shift[across:2 * across] = lane_shift

    def spread(columns):
        return (iota((wide, columns), 0) // S8 == iota((wide, columns), 1)).astype(F32)

    def same_slot():
        return iota((wide, wide), 0) % S8 == iota((wide, wide), 1) % S8

    def store_parts(x, g, v):
        high, low = split(v.reshape(wide, across))
        parts[x, 0:wide, g * across:(g + 1) * across] = high
        parts[x, wide:2 * wide, g * across:(g + 1) * across] = low

    def add_gram(x):
        acc[...] += dot_nt(parts[x, 0:wide, :], parts[x])

    acc[...] = jnp.zeros_like(acc)

    def load_row(x, c):
        for g in range(groups):
            z = slice(g * S8, (g + 1) * S8)
            v = mask[x + 1, z][None] * u[x, :, z, :]
            v0[x + 1, :, z, :] = v
            store_parts(x, g, v)
        add_gram(x)
        return c

    def fetch_row(x, c):
        fetch(x).wait()
        return load_row(x, c)

    lax.fori_loop(1, rows - 1, fetch_row, 0)
    load_row(0, 0)
    load_row(rows - 1, 0)

    def gram_copy(r, d):
        return pltpu.make_async_remote_copy(
            src_ref=gsend.at[r], dst_ref=gbuf.at[r, d], send_sem=g_send.at[r, d], recv_sem=g_recv.at[r, d],
            device_id={"gx": lax.rem(me + d, n)}, device_id_type=MESH)

    def gram_start(r):
        same = same_slot()
        e_t = (iota((channels, wide), 0) == iota((channels, wide), 1) // S8).astype(F32)
        e = spread(across)
        hh = dot_nn(dot_nn(e_t, jnp.where(same, acc[:, 0:wide], 0.0), HI), e, HI)
        hl = dot_nn(dot_nn(e_t, jnp.where(same, acc[:, wide:2 * wide], 0.0), HI), e, HI)
        eye = (iota((channels, channels), 0) == iota((channels, channels), 1)).astype(F32)
        eye_wide = (iota((channels, across), 0) == iota((channels, across), 1)).astype(F32)
        lh = lax.dot_general(hl[:, 0:channels], eye_wide, (((0,), (0,)), ((), ())), precision=HI,
                             preferred_element_type=F32)
        whole = hh + hl + lh
        packed = whole[0:S8]
        for b in range(1, channels // S8):
            packed = packed + pltpu.roll(whole[b * S8:(b + 1) * S8], channels * b, 1)
        gsend[r] = packed
        lax.fori_loop(1, n, lambda d, c: (gram_copy(r, d).start(), c)[1], 0)

    def gram_end(r):
        def body(d, c):
            gram_copy(r, d).wait()
            return c

        lax.fori_loop(1, n, body, 0)

        def add(d, total):
            return total + gbuf[r, d]

        total = lax.fori_loop(1, n, add, gsend[r])
        blocks = [total[:, 0:channels]]
        for b in range(1, channels // S8):
            blocks.append(pltpu.roll(total, across - channels * b, 1)[:, 0:channels])
        return jnp.concatenate(blocks, axis=0) / count

    def mixing(g, beta):
        row, col = iota((channels, channels), 0), iota((channels, channels), 1)
        low = row >= col
        excess = g - (row == col).astype(F32)
        q = jnp.where(low, beta + 1.0 * excess, 0.0)
        e = spread(channels)
        big = jnp.where(same_slot(), -dot_nt(dot_nn(e, q, HI), e, HI), 0.0)
        high, rest = split(big)
        mix[:, 0:wide] = high
        mix[:, wide:2 * wide] = high
        mix[:, 2 * wide:3 * wide] = rest
        return beta + 0.5 * jnp.where(low, excess, 0.0)

    sub = iota((1, S8, across), 1)

    def advance_row(v, x, write):
        zero = jnp.zeros((channels, S8, across), F32)
        pairs = 2
        for g0 in range(0, groups, pairs):
            cols = slice(g0 * across, (g0 + pairs) * across)
            mixed = dot_nn(mix[:, 0:2 * wide], parts[x, :, cols]) + dot_nn(mix[:, 2 * wide:], parts[x, 0:wide, cols])
            sides = []
            for g in range(g0, g0 + pairs):
                own = slice(g * across, (g + 1) * across)
                sides.append(dot_nn(parts[x, 0:wide, own], shift[0:across])
                             + dot_nn(parts[x, wide:2 * wide, own], shift[across:2 * across]))
            for i, g in enumerate(range(g0, g0 + pairs)):
                z = slice(g * S8, (g + 1) * S8)
                core = v[x + 1, :, z, :]
                before = v[x + 1, :, (g - 1) * S8:g * S8, :] if g > 0 else zero
                after = v[x + 1, :, (g + 1) * S8:(g + 2) * S8, :] if g < groups - 1 else zero
                up = pltpu.roll(jnp.where(sub == S8 - 1, before, core), 1, 1)
                down = pltpu.roll(jnp.where(sub == 0, after, core), S8 - 1, 1)
                total = (mixed[:, i * across:(i + 1) * across] + sides[i]).reshape(channels, S8, across)
                total = total + up + down + v[x, :, z, :] + v[x + 2, :, z, :]
                new = keep[x, z][None] * core + (0.1 * mask[x + 1, z])[None] * total
                write(x, g, z, new)

    def write_first(x, g, z, new):
        v1[x + 1, :, z, :] = new
        store_parts(x, g, new)

    def write_last(x, g, z, new):
        u[x, :, z, :] = jnp.where(mask[x + 1, z][None] > 0.5, new, u[x, :, z, :])

    gram_start(0)

    @pl.when(me > 0)
    def _():
        u_l[1].start()

    @pl.when(me < n - 1)
    def _():
        u_r[1].start()

    @pl.when(me > 0)
    def _():
        mask_r.wait_recv()

    @pl.when(me < n - 1)
    def _():
        mask_l.wait_recv()

    zi, yi = iota((depth, across), 0), iota((depth, across), 1)

    def weigh(x, c):
        m = mask[x + 1]
        near = mask[x] + mask[x + 2]
        near = near + jnp.where(yi == 0, 0.0, pltpu.roll(m, 1, 1))
        near = near + jnp.where(yi == across - 1, 0.0, pltpu.roll(m, across - 1, 1))
        near = near + jnp.where(zi == 0, 0.0, pltpu.roll(m, 1, 0))
        near = near + jnp.where(zi == depth - 1, 0.0, pltpu.roll(m, depth - 1, 0))
        keep[x] = m * (1.0 - 0.1 * near)
        return c

    lax.fori_loop(0, rows, weigh, 0)

    beta = mixing(gram_end(0), duals[...])
    acc[...] = jnp.zeros_like(acc)

    def first(x, c):
        advance_row(v0, x, write_first)
        add_gram(x)
        return c

    lax.fori_loop(1, rows - 1, first, 0)

    @pl.when(me > 0)
    def _():
        u_r[0].wait_recv()
        u_r[1].wait_recv()
        v0[0] = v0[0] * mask[0][None]

    first(0, 0)

    @pl.when(me < n - 1)
    def _():
        u_l[0].wait_recv()
        u_l[1].wait_recv()
        v0[last] = v0[last] * mask[last][None]

    first(rows - 1, 0)

    gram_start(1)

    @pl.when(me > 0)
    def _():
        w_l.start()

    @pl.when(me < n - 1)
    def _():
        w_r.start()

    beta = mixing(gram_end(1), beta)
    duals_out[...] = beta

    def store(x):
        return pltpu.make_async_copy(u.at[x], out.at[:, x], out_sem.at[x])

    def second(x, c):
        advance_row(v1, x, write_last)
        store(x).start()
        return c

    lax.fori_loop(1, rows - 1, second, 0)

    @pl.when(me > 0)
    def _():
        mask_l.wait_send()
        u_l[0].wait_send()
        u_l[1].wait_send()
        w_r.wait_recv()

    @pl.when(me < n - 1)
    def _():
        mask_r.wait_send()
        u_r[0].wait_send()
        u_r[1].wait_send()
        w_l.wait_recv()

    second(0, 0)
    second(rows - 1, 0)

    @pl.when(me > 0)
    def _():
        w_l.wait_send()

    @pl.when(me < n - 1)
    def _():
        w_r.wait_send()

    lax.fori_loop(0, rows, lambda x, c: (store(x).wait(), c)[1], 0)


def per_device(field, occupancy, duals):
    channels, rows, depth, across = field.shape
    n = lax.axis_size("gx")
    wide = channels * S8
    vmem = pl.BlockSpec(memory_space=pltpu.VMEM)
    dma = pltpu.SemaphoreType.DMA
    return pl.pallas_call(
        functools.partial(kernel, n),
        out_shape=(jax.ShapeDtypeStruct(field.shape, F32), jax.ShapeDtypeStruct(duals.shape, F32)),
        in_specs=[pl.BlockSpec(memory_space=pl.ANY), vmem, vmem],
        out_specs=(pl.BlockSpec(memory_space=pl.ANY), vmem),
        scratch_shapes=[
            pltpu.VMEM((rows, channels, depth, across), F32),
            pltpu.VMEM((rows + 2, channels, depth, across), F32),
            pltpu.VMEM((rows + 2, channels, depth, across), F32),
            pltpu.VMEM((rows, 2 * wide, depth // S8 * across), BF16),
            pltpu.VMEM((rows + 2, depth, across), F32),
            pltpu.VMEM((rows, depth, across), F32),
            pltpu.VMEM((wide, 2 * wide), F32),
            pltpu.VMEM((wide, 3 * wide), BF16),
            pltpu.VMEM((2 * across, across), BF16),
            pltpu.VMEM((2, S8, across), F32),
            pltpu.VMEM((2, n, S8, across), F32),
            dma((rows,)), dma((rows,)), dma((6,)), dma((6,)), dma((2,)), dma((2,)), dma((2, n)), dma((2, n)),
        ],
        compiler_params=pltpu.CompilerParams(
            collective_id=0, has_side_effects=True, vmem_limit_bytes=56 * 1024 * 1024),
    )(field, occupancy, duals)


def solution(mesh):
    placed = (
        P(None, ("world", "gx"), None, None),
        P(("world", "gx"), None, None),
        P("world", None),
    )
    return jax.shard_map(
        per_device,
        mesh=mesh,
        in_specs=placed,
        out_specs=(P(None, ("world", "gx"), None, None), P("world", None)),
        check_vma=False,
    )
```

```python
import functools

import jax
import jax.numpy as jnp
from jax import lax
from jax.experimental import pallas as pl
from jax.experimental.pallas import tpu as pltpu
from jax.sharding import PartitionSpec as P

MESH = pl.DeviceIdType.MESH
HI = lax.Precision.HIGHEST
S8 = 8
F32 = jnp.float32
BF16 = jnp.bfloat16


def iota(shape, dim):
    return lax.broadcasted_iota(jnp.int32, shape, dim)


def dot_nt(a, b, precision=None):
    return lax.dot_general(a, b, (((1,), (1,)), ((), ())), precision=precision, preferred_element_type=F32)


def dot_nn(a, b, precision=None):
    return lax.dot_general(a, b, (((1,), (0,)), ((), ())), precision=precision, preferred_element_type=F32)


def split(x):
    high = x.astype(BF16)
    return high, (x - high.astype(F32)).astype(BF16)


def kernel(n, field, occ, duals, u, duals_out, v0, v1, parts, mask, keep, acc, mix, shift,
           gsend, gbuf, in_sem, h_send, h_recv, m_send, m_recv, g_send, g_recv):
    me = lax.axis_index("gx")
    rows, channels, depth, across = u.shape
    wide = channels * S8
    groups = depth // S8
    count = n * rows * depth * across
    last = rows + 1

    barrier = pltpu.get_barrier_semaphore()

    def greet(d, c):
        pl.semaphore_signal(barrier, inc=1, device_id={"gx": lax.rem(me + d, n)}, device_id_type=MESH)
        return c

    lax.fori_loop(1, n, greet, 0)

    def fetch(x):
        return pltpu.make_async_copy(field.at[:, x], u.at[x], in_sem.at[x])

    fetch(0).start()
    fetch(rows - 1).start()
    for x in range(1, rows - 1):
        fetch(x).start()

    for x in range(rows):
        mask[x + 1] = occ[x].astype(F32)

    @pl.when(me == 0)
    def _():
        mask[0] = jnp.zeros((depth, across), F32)
        v0[0] = jnp.zeros((channels, depth, across), F32)
        v1[0] = jnp.zeros((channels, depth, across), F32)

    @pl.when(me == n - 1)
    def _():
        mask[last] = jnp.zeros((depth, across), F32)
        v0[last] = jnp.zeros((channels, depth, across), F32)
        v1[last] = jnp.zeros((channels, depth, across), F32)

    def to_left(src, dst, send, recv):
        return pltpu.make_async_remote_copy(src_ref=src, dst_ref=dst, send_sem=send, recv_sem=recv,
                                            device_id={"gx": me - 1}, device_id_type=MESH)

    def to_right(src, dst, send, recv):
        return pltpu.make_async_remote_copy(src_ref=src, dst_ref=dst, send_sem=send, recv_sem=recv,
                                            device_id={"gx": me + 1}, device_id_type=MESH)

    mask_l = to_left(mask.at[1], mask.at[last], m_send.at[0], m_recv.at[0])
    mask_r = to_right(mask.at[rows], mask.at[0], m_send.at[1], m_recv.at[1])
    cut = channels * 3 // 8
    pieces = (pl.ds(0, cut), pl.ds(cut, channels - cut))
    u_l = [to_left(u.at[0, p], v0.at[last, p], h_send.at[i], h_recv.at[i]) for i, p in enumerate(pieces)]
    u_r = [to_right(u.at[rows - 1, p], v0.at[0, p], h_send.at[2 + i], h_recv.at[2 + i]) for i, p in enumerate(pieces)]
    w_l = to_left(v1.at[1], v1.at[last], h_send.at[4], h_recv.at[4])
    w_r = to_right(v1.at[rows], v1.at[0], h_send.at[5], h_recv.at[5])

    pl.semaphore_wait(barrier, n - 1)

    @pl.when(me > 0)
    def _():
        mask_l.start()

    @pl.when(me < n - 1)
    def _():
        mask_r.start()

    fetch(0).wait()

    @pl.when(me > 0)
    def _():
        u_l[0].start()

    fetch(rows - 1).wait()

    @pl.when(me < n - 1)
    def _():
        u_r[0].start()

    lane_shift = (jnp.abs(iota((across, across), 0) - iota((across, across), 1)) == 1).astype(F32).astype(BF16)
    shift[0:across] = lane_shift
    shift[across:2 * across] = lane_shift

    def spread(columns):
        return (iota((wide, columns), 0) // S8 == iota((wide, columns), 1)).astype(F32)

    def same_slot():
        return iota((wide, wide), 0) % S8 == iota((wide, wide), 1) % S8

    def store_parts(x, g, v):
        high, low = split(v.reshape(wide, across))
        parts[x, 0:wide, g * across:(g + 1) * across] = high
        parts[x, wide:2 * wide, g * across:(g + 1) * across] = low

    def add_gram(x):
        acc[...] += dot_nt(parts[x, 0:wide, :], parts[x])

    acc[...] = jnp.zeros_like(acc)

    def load_row(x, c):
        for g in range(groups):
            z = slice(g * S8, (g + 1) * S8)
            v = mask[x + 1, z][None] * u[x, :, z, :]
            v0[x + 1, :, z, :] = v
            store_parts(x, g, v)
        add_gram(x)
        return c

    def fetch_row(x, c):
        fetch(x).wait()
        return load_row(x, c)

    lax.fori_loop(1, rows - 1, fetch_row, 0)
    load_row(0, 0)
    load_row(rows - 1, 0)

    def gram_copy(r, d):
        return pltpu.make_async_remote_copy(
            src_ref=gsend.at[r], dst_ref=gbuf.at[r, d], send_sem=g_send.at[r, d], recv_sem=g_recv.at[r, d],
            device_id={"gx": lax.rem(me + d, n)}, device_id_type=MESH)

    def gram_start(r):
        same = same_slot()
        e_t = (iota((channels, wide), 0) == iota((channels, wide), 1) // S8).astype(F32)
        e = spread(across)
        hh = dot_nn(dot_nn(e_t, jnp.where(same, acc[:, 0:wide], 0.0), HI), e, HI)
        hl = dot_nn(dot_nn(e_t, jnp.where(same, acc[:, wide:2 * wide], 0.0), HI), e, HI)
        eye = (iota((channels, channels), 0) == iota((channels, channels), 1)).astype(F32)
        eye_wide = (iota((channels, across), 0) == iota((channels, across), 1)).astype(F32)
        lh = lax.dot_general(hl[:, 0:channels], eye_wide, (((0,), (0,)), ((), ())), precision=HI,
                             preferred_element_type=F32)
        whole = hh + hl + lh
        packed = whole[0:S8]
        for b in range(1, channels // S8):
            packed = packed + pltpu.roll(whole[b * S8:(b + 1) * S8], channels * b, 1)
        gsend[r] = packed
        lax.fori_loop(1, n, lambda d, c: (gram_copy(r, d).start(), c)[1], 0)

    def gram_end(r):
        def body(d, c):
            gram_copy(r, d).wait()
            return c

        lax.fori_loop(1, n, body, 0)

        def add(d, total):
            return total + gbuf[r, d]

        total = lax.fori_loop(1, n, add, gsend[r])
        blocks = [total[:, 0:channels]]
        for b in range(1, channels // S8):
            blocks.append(pltpu.roll(total, across - channels * b, 1)[:, 0:channels])
        return jnp.concatenate(blocks, axis=0) / count

    def mixing(g, beta):
        row, col = iota((channels, channels), 0), iota((channels, channels), 1)
        low = row >= col
        excess = g - (row == col).astype(F32)
        q = jnp.where(low, beta + 1.0 * excess, 0.0)
        e = spread(channels)
        big = jnp.where(same_slot(), -dot_nt(dot_nn(e, q, HI), e, HI), 0.0)
        high, rest = split(big)
        mix[:, 0:wide] = high
        mix[:, wide:2 * wide] = high
        mix[:, 2 * wide:3 * wide] = rest
        return beta + 0.5 * jnp.where(low, excess, 0.0)

    sub = iota((1, S8, across), 1)

    def advance_row(v, x, write):
        zero = jnp.zeros((channels, S8, across), F32)
        pairs = 2
        for g0 in range(0, groups, pairs):
            cols = slice(g0 * across, (g0 + pairs) * across)
            mixed = dot_nn(mix[:, 0:2 * wide], parts[x, :, cols]) + dot_nn(mix[:, 2 * wide:], parts[x, 0:wide, cols])
            sides = []
            for g in range(g0, g0 + pairs):
                own = slice(g * across, (g + 1) * across)
                sides.append(dot_nn(parts[x, 0:wide, own], shift[0:across])
                             + dot_nn(parts[x, wide:2 * wide, own], shift[across:2 * across]))
            for i, g in enumerate(range(g0, g0 + pairs)):
                z = slice(g * S8, (g + 1) * S8)
                core = v[x + 1, :, z, :]
                before = v[x + 1, :, (g - 1) * S8:g * S8, :] if g > 0 else zero
                after = v[x + 1, :, (g + 1) * S8:(g + 2) * S8, :] if g < groups - 1 else zero
                up = pltpu.roll(jnp.where(sub == S8 - 1, before, core), 1, 1)
                down = pltpu.roll(jnp.where(sub == 0, after, core), S8 - 1, 1)
                total = (mixed[:, i * across:(i + 1) * across] + sides[i]).reshape(channels, S8, across)
                total = total + up + down + v[x, :, z, :] + v[x + 2, :, z, :]
                new = keep[x, z][None] * core + (0.1 * mask[x + 1, z])[None] * total
                write(x, g, z, new)

    def write_first(x, g, z, new):
        v1[x + 1, :, z, :] = new
        store_parts(x, g, new)

    def write_last(x, g, z, new):
        u[x, :, z, :] = jnp.where(mask[x + 1, z][None] > 0.5, new, u[x, :, z, :])

    gram_start(0)

    @pl.when(me > 0)
    def _():
        u_l[1].start()

    @pl.when(me < n - 1)
    def _():
        u_r[1].start()

    @pl.when(me > 0)
    def _():
        mask_r.wait_recv()

    @pl.when(me < n - 1)
    def _():
        mask_l.wait_recv()

    zi, yi = iota((depth, across), 0), iota((depth, across), 1)

    def weigh(x, c):
        m = mask[x + 1]
        near = mask[x] + mask[x + 2]
        near = near + jnp.where(yi == 0, 0.0, pltpu.roll(m, 1, 1))
        near = near + jnp.where(yi == across - 1, 0.0, pltpu.roll(m, across - 1, 1))
        near = near + jnp.where(zi == 0, 0.0, pltpu.roll(m, 1, 0))
        near = near + jnp.where(zi == depth - 1, 0.0, pltpu.roll(m, depth - 1, 0))
        keep[x] = m * (1.0 - 0.1 * near)
        return c

    lax.fori_loop(0, rows, weigh, 0)

    beta = mixing(gram_end(0), duals[...])
    acc[...] = jnp.zeros_like(acc)

    def first(x, c):
        advance_row(v0, x, write_first)
        add_gram(x)
        return c

    lax.fori_loop(1, rows - 1, first, 0)

    @pl.when(me > 0)
    def _():
        u_r[0].wait_recv()
        u_r[1].wait_recv()
        v0[0] = v0[0] * mask[0][None]

    first(0, 0)

    @pl.when(me < n - 1)
    def _():
        u_l[0].wait_recv()
        u_l[1].wait_recv()
        v0[last] = v0[last] * mask[last][None]

    first(rows - 1, 0)

    gram_start(1)

    @pl.when(me > 0)
    def _():
        w_l.start()

    @pl.when(me < n - 1)
    def _():
        w_r.start()

    beta = mixing(gram_end(1), beta)
    duals_out[...] = beta

    def second(x, c):
        advance_row(v1, x, write_last)
        return c

    lax.fori_loop(1, rows - 1, second, 0)

    @pl.when(me > 0)
    def _():
        mask_l.wait_send()
        u_l[0].wait_send()
        u_l[1].wait_send()
        w_r.wait_recv()

    @pl.when(me < n - 1)
    def _():
        mask_r.wait_send()
        u_r[0].wait_send()
        u_r[1].wait_send()
        w_l.wait_recv()

    second(0, 0)
    second(rows - 1, 0)

    @pl.when(me > 0)
    def _():
        w_l.wait_send()

    @pl.when(me < n - 1)
    def _():
        w_r.wait_send()


def per_device(field, occupancy, duals):
    channels, rows, depth, across = field.shape
    n = lax.axis_size("gx")
    wide = channels * S8
    vmem = pl.BlockSpec(memory_space=pltpu.VMEM)
    dma = pltpu.SemaphoreType.DMA
    held, beta = pl.pallas_call(
        functools.partial(kernel, n),
        out_shape=(pltpu.VMEM((rows, channels, depth, across), F32), jax.ShapeDtypeStruct(duals.shape, F32)),
        in_specs=[pl.BlockSpec(memory_space=pl.ANY), vmem, vmem],
        out_specs=(vmem, vmem),
        scratch_shapes=[
            pltpu.VMEM((rows + 2, channels, depth, across), F32),
            pltpu.VMEM((rows + 2, channels, depth, across), F32),
            pltpu.VMEM((rows, 2 * wide, depth // S8 * across), BF16),
            pltpu.VMEM((rows + 2, depth, across), F32),
            pltpu.VMEM((rows, depth, across), F32),
            pltpu.VMEM((wide, 2 * wide), F32),
            pltpu.VMEM((wide, 3 * wide), BF16),
            pltpu.VMEM((2 * across, across), BF16),
            pltpu.VMEM((2, S8, across), F32),
            pltpu.VMEM((2, n, S8, across), F32),
            dma((rows,)), dma((6,)), dma((6,)), dma((2,)), dma((2,)), dma((2, n)), dma((2, n)),
        ],
        compiler_params=pltpu.CompilerParams(
            collective_id=0, has_side_effects=True, vmem_limit_bytes=40 * 1024 * 1024),
    )(field, occupancy, duals)
    result = jnp.transpose(held, (1, 0, 2, 3))
    return result, beta


def solution(mesh):
    placed = (
        P(None, ("world", "gx"), None, None),
        P(("world", "gx"), None, None),
        P("world", None),
    )
    return jax.shard_map(
        per_device,
        mesh=mesh,
        in_specs=placed,
        out_specs=(P(None, ("world", "gx"), None, None), P("world", None)),
        check_vma=False,
    )
```

```python
import functools

import jax
import jax.numpy as jnp
from jax import lax
from jax.experimental import pallas as pl
from jax.experimental.pallas import tpu as pltpu
from jax.sharding import PartitionSpec as P

MESH = pl.DeviceIdType.MESH
HI = lax.Precision.HIGHEST
S8 = 8
F32 = jnp.float32
BF16 = jnp.bfloat16


def iota(shape, dim):
    return lax.broadcasted_iota(jnp.int32, shape, dim)


def dot_nt(a, b, precision=None):
    return lax.dot_general(a, b, (((1,), (1,)), ((), ())), precision=precision, preferred_element_type=F32)


def dot_nn(a, b, precision=None):
    return lax.dot_general(a, b, (((1,), (0,)), ((), ())), precision=precision, preferred_element_type=F32)


def split(x):
    high = x.astype(BF16)
    return high, (x - high.astype(F32)).astype(BF16)


def kernel(n, field, occ, duals, u, duals_out, v0, v1, parts, mask, keep, acc, mix, shift,
           gsend, gbuf, in_sem, h_send, h_recv, m_send, m_recv, g_send, g_recv):
    me = lax.axis_index("gx")
    rows, channels, depth, across = u.shape
    wide = channels * S8
    groups = depth // S8
    count = n * rows * depth * across
    last = rows + 1

    barrier = pltpu.get_barrier_semaphore()

    def greet(d, c):
        pl.semaphore_signal(barrier, inc=1, device_id={"gx": lax.rem(me + d, n)}, device_id_type=MESH)
        return c

    lax.fori_loop(1, n, greet, 0)

    def fetch(x):
        return pltpu.make_async_copy(field.at[:, x], u.at[x], in_sem.at[x])

    fetch(0).start()
    fetch(rows - 1).start()
    for x in range(1, rows - 1):
        fetch(x).start()

    for x in range(rows):
        mask[x + 1] = occ[x].astype(F32)

    @pl.when(me == 0)
    def _():
        mask[0] = jnp.zeros((depth, across), F32)
        v0[0] = jnp.zeros((channels, depth, across), F32)
        v1[0] = jnp.zeros((channels, depth, across), F32)

    @pl.when(me == n - 1)
    def _():
        mask[last] = jnp.zeros((depth, across), F32)
        v0[last] = jnp.zeros((channels, depth, across), F32)
        v1[last] = jnp.zeros((channels, depth, across), F32)

    def to_left(src, dst, send, recv):
        return pltpu.make_async_remote_copy(src_ref=src, dst_ref=dst, send_sem=send, recv_sem=recv,
                                            device_id={"gx": me - 1}, device_id_type=MESH)

    def to_right(src, dst, send, recv):
        return pltpu.make_async_remote_copy(src_ref=src, dst_ref=dst, send_sem=send, recv_sem=recv,
                                            device_id={"gx": me + 1}, device_id_type=MESH)

    mask_l = to_left(mask.at[1], mask.at[last], m_send.at[0], m_recv.at[0])
    mask_r = to_right(mask.at[rows], mask.at[0], m_send.at[1], m_recv.at[1])
    cut = channels * 2 // 8
    pieces = (pl.ds(0, cut), pl.ds(cut, channels - cut))
    u_l = [to_left(u.at[0, p], v0.at[last, p], h_send.at[i], h_recv.at[i]) for i, p in enumerate(pieces)]
    u_r = [to_right(u.at[rows - 1, p], v0.at[0, p], h_send.at[2 + i], h_recv.at[2 + i]) for i, p in enumerate(pieces)]
    w_l = to_left(v1.at[1], v1.at[last], h_send.at[4], h_recv.at[4])
    w_r = to_right(v1.at[rows], v1.at[0], h_send.at[5], h_recv.at[5])

    pl.semaphore_wait(barrier, n - 1)

    @pl.when(me > 0)
    def _():
        mask_l.start()

    @pl.when(me < n - 1)
    def _():
        mask_r.start()

    fetch(0).wait()

    @pl.when(me > 0)
    def _():
        u_l[0].start()

    fetch(rows - 1).wait()

    @pl.when(me < n - 1)
    def _():
        u_r[0].start()

    lane_shift = (jnp.abs(iota((across, across), 0) - iota((across, across), 1)) == 1).astype(F32).astype(BF16)
    shift[0:across] = lane_shift
    shift[across:2 * across] = lane_shift

    def spread(columns):
        return (iota((wide, columns), 0) // S8 == iota((wide, columns), 1)).astype(F32)

    def same_slot():
        return iota((wide, wide), 0) % S8 == iota((wide, wide), 1) % S8

    def store_parts(x, g, v):
        high, low = split(v.reshape(wide, across))
        parts[x, 0:wide, g * across:(g + 1) * across] = high
        parts[x, wide:2 * wide, g * across:(g + 1) * across] = low

    def add_gram(x):
        acc[...] += dot_nt(parts[x, 0:wide, :], parts[x])

    acc[...] = jnp.zeros_like(acc)

    def load_row(x, c):
        for g in range(groups):
            z = slice(g * S8, (g + 1) * S8)
            v = mask[x + 1, z][None] * u[x, :, z, :]
            v0[x + 1, :, z, :] = v
            store_parts(x, g, v)
        add_gram(x)
        return c

    def fetch_row(x, c):
        fetch(x).wait()
        return load_row(x, c)

    lax.fori_loop(1, rows - 1, fetch_row, 0)
    load_row(0, 0)
    load_row(rows - 1, 0)

    def gram_copy(r, d):
        return pltpu.make_async_remote_copy(
            src_ref=gsend.at[r], dst_ref=gbuf.at[r, d], send_sem=g_send.at[r, d], recv_sem=g_recv.at[r, d],
            device_id={"gx": lax.rem(me + d, n)}, device_id_type=MESH)

    def gram_start(r):
        same = same_slot()
        e_t = (iota((channels, wide), 0) == iota((channels, wide), 1) // S8).astype(F32)
        e = spread(across)
        hh = dot_nn(dot_nn(e_t, jnp.where(same, acc[:, 0:wide], 0.0), HI), e, HI)
        hl = dot_nn(dot_nn(e_t, jnp.where(same, acc[:, wide:2 * wide], 0.0), HI), e, HI)
        eye = (iota((channels, channels), 0) == iota((channels, channels), 1)).astype(F32)
        eye_wide = (iota((channels, across), 0) == iota((channels, across), 1)).astype(F32)
        lh = lax.dot_general(hl[:, 0:channels], eye_wide, (((0,), (0,)), ((), ())), precision=HI,
                             preferred_element_type=F32)
        whole = hh + hl + lh
        packed = whole[0:S8]
        for b in range(1, channels // S8):
            packed = packed + pltpu.roll(whole[b * S8:(b + 1) * S8], channels * b, 1)
        gsend[r] = packed
        lax.fori_loop(1, n, lambda d, c: (gram_copy(r, d).start(), c)[1], 0)

    def gram_end(r):
        def body(d, c):
            gram_copy(r, d).wait()
            return c

        lax.fori_loop(1, n, body, 0)

        def add(d, total):
            return total + gbuf[r, d]

        total = lax.fori_loop(1, n, add, gsend[r])
        blocks = [total[:, 0:channels]]
        for b in range(1, channels // S8):
            blocks.append(pltpu.roll(total, across - channels * b, 1)[:, 0:channels])
        return jnp.concatenate(blocks, axis=0) / count

    def mixing(g, beta):
        row, col = iota((channels, channels), 0), iota((channels, channels), 1)
        low = row >= col
        excess = g - (row == col).astype(F32)
        q = jnp.where(low, beta + 1.0 * excess, 0.0)
        e = spread(channels)
        big = jnp.where(same_slot(), -dot_nt(dot_nn(e, q, HI), e, HI), 0.0)
        high, rest = split(big)
        mix[:, 0:wide] = high
        mix[:, wide:2 * wide] = high
        mix[:, 2 * wide:3 * wide] = rest
        return beta + 0.5 * jnp.where(low, excess, 0.0)

    sub = iota((1, S8, across), 1)

    def advance_row(v, x, write):
        zero = jnp.zeros((channels, S8, across), F32)
        pairs = 2
        for g0 in range(0, groups, pairs):
            cols = slice(g0 * across, (g0 + pairs) * across)
            mixed = dot_nn(mix[:, 0:2 * wide], parts[x, :, cols]) + dot_nn(mix[:, 2 * wide:], parts[x, 0:wide, cols])
            sides = []
            for g in range(g0, g0 + pairs):
                own = slice(g * across, (g + 1) * across)
                sides.append(dot_nn(parts[x, 0:wide, own], shift[0:across])
                             + dot_nn(parts[x, wide:2 * wide, own], shift[across:2 * across]))
            for i, g in enumerate(range(g0, g0 + pairs)):
                z = slice(g * S8, (g + 1) * S8)
                core = v[x + 1, :, z, :]
                before = v[x + 1, :, (g - 1) * S8:g * S8, :] if g > 0 else zero
                after = v[x + 1, :, (g + 1) * S8:(g + 2) * S8, :] if g < groups - 1 else zero
                up = pltpu.roll(jnp.where(sub == S8 - 1, before, core), 1, 1)
                down = pltpu.roll(jnp.where(sub == 0, after, core), S8 - 1, 1)
                total = (mixed[:, i * across:(i + 1) * across] + sides[i]).reshape(channels, S8, across)
                total = total + up + down + v[x, :, z, :] + v[x + 2, :, z, :]
                new = keep[x, z][None] * core + (0.1 * mask[x + 1, z])[None] * total
                write(x, g, z, new)

    def write_first(x, g, z, new):
        v1[x + 1, :, z, :] = new
        store_parts(x, g, new)

    def write_last(x, g, z, new):
        u[x, :, z, :] = jnp.where(mask[x + 1, z][None] > 0.5, new, u[x, :, z, :])

    gram_start(0)

    @pl.when(me > 0)
    def _():
        u_l[1].start()

    @pl.when(me < n - 1)
    def _():
        u_r[1].start()

    @pl.when(me > 0)
    def _():
        mask_r.wait_recv()

    @pl.when(me < n - 1)
    def _():
        mask_l.wait_recv()

    zi, yi = iota((depth, across), 0), iota((depth, across), 1)

    def weigh(x, c):
        m = mask[x + 1]
        near = mask[x] + mask[x + 2]
        near = near + jnp.where(yi == 0, 0.0, pltpu.roll(m, 1, 1))
        near = near + jnp.where(yi == across - 1, 0.0, pltpu.roll(m, across - 1, 1))
        near = near + jnp.where(zi == 0, 0.0, pltpu.roll(m, 1, 0))
        near = near + jnp.where(zi == depth - 1, 0.0, pltpu.roll(m, depth - 1, 0))
        keep[x] = m * (1.0 - 0.1 * near)
        return c

    lax.fori_loop(0, rows, weigh, 0)

    beta = mixing(gram_end(0), duals[...])
    acc[...] = jnp.zeros_like(acc)

    def first(x, c):
        advance_row(v0, x, write_first)
        add_gram(x)
        return c

    lax.fori_loop(1, rows - 1, first, 0)

    @pl.when(me > 0)
    def _():
        u_r[0].wait_recv()
        u_r[1].wait_recv()
        v0[0] = v0[0] * mask[0][None]

    first(0, 0)

    @pl.when(me < n - 1)
    def _():
        u_l[0].wait_recv()
        u_l[1].wait_recv()
        v0[last] = v0[last] * mask[last][None]

    first(rows - 1, 0)

    gram_start(1)

    @pl.when(me > 0)
    def _():
        w_l.start()

    @pl.when(me < n - 1)
    def _():
        w_r.start()

    beta = mixing(gram_end(1), beta)
    duals_out[...] = beta

    def second(x, c):
        advance_row(v1, x, write_last)
        return c

    lax.fori_loop(1, rows - 1, second, 0)

    @pl.when(me > 0)
    def _():
        mask_l.wait_send()
        u_l[0].wait_send()
        u_l[1].wait_send()
        w_r.wait_recv()

    @pl.when(me < n - 1)
    def _():
        mask_r.wait_send()
        u_r[0].wait_send()
        u_r[1].wait_send()
        w_l.wait_recv()

    second(0, 0)
    second(rows - 1, 0)

    @pl.when(me > 0)
    def _():
        w_l.wait_send()

    @pl.when(me < n - 1)
    def _():
        w_r.wait_send()


def per_device(field, occupancy, duals):
    channels, rows, depth, across = field.shape
    n = lax.axis_size("gx")
    wide = channels * S8
    vmem = pl.BlockSpec(memory_space=pltpu.VMEM)
    dma = pltpu.SemaphoreType.DMA
    held, beta = pl.pallas_call(
        functools.partial(kernel, n),
        out_shape=(pltpu.VMEM((rows, channels, depth, across), F32), jax.ShapeDtypeStruct(duals.shape, F32)),
        in_specs=[pl.BlockSpec(memory_space=pl.ANY), vmem, vmem],
        out_specs=(vmem, vmem),
        scratch_shapes=[
            pltpu.VMEM((rows + 2, channels, depth, across), F32),
            pltpu.VMEM((rows + 2, channels, depth, across), F32),
            pltpu.VMEM((rows, 2 * wide, depth // S8 * across), BF16),
            pltpu.VMEM((rows + 2, depth, across), F32),
            pltpu.VMEM((rows, depth, across), F32),
            pltpu.VMEM((wide, 2 * wide), F32),
            pltpu.VMEM((wide, 3 * wide), BF16),
            pltpu.VMEM((2 * across, across), BF16),
            pltpu.VMEM((2, S8, across), F32),
            pltpu.VMEM((2, n, S8, across), F32),
            dma((rows,)), dma((6,)), dma((6,)), dma((2,)), dma((2,)), dma((2, n)), dma((2, n)),
        ],
        compiler_params=pltpu.CompilerParams(
            collective_id=0, has_side_effects=True, vmem_limit_bytes=40 * 1024 * 1024),
    )(field, occupancy, duals)
    result = jnp.transpose(held, (1, 0, 2, 3))
    return result, beta


def solution(mesh):
    placed = (
        P(None, ("world", "gx"), None, None),
        P(("world", "gx"), None, None),
        P("world", None),
    )
    return jax.shard_map(
        per_device,
        mesh=mesh,
        in_specs=placed,
        out_specs=(P(None, ("world", "gx"), None, None), P("world", None)),
        check_vma=False,
    )
```
